32 devices in a mesh: groups: 2 (over y), batch: 4 (over z), blk: 2 (over x), sub: 2 (over core).
Axes of the slice: x: 2, y: 2, z: 4, core: 2. Of those that a mesh axis runs over, the one named last changes fastest.
Arguments:
- density: bfloat16 [1024, 512], P(('groups', 'blk', 'sub')), parts along dimension 0, as said below
- block_home: int32 [32], P('groups'), parts along dimension 0, may hold values from 0 to 15, as said below
- significant: int32 [32, 16], P(('groups', 'batch', 'blk', 'sub')), parts along dimension 0, may hold values from 0 to 15, as said below
- points: float32 [3, 32768], P(None, ('groups', 'batch', 'blk', 'sub')), parts along dimension 1, may hold values from -2 to 2
- weights: float32 [32768], P(('groups', 'batch', 'blk', 'sub')), parts along dimension 0, may hold values from 0.00048828125 to 0.0048828125
- centers: float32 [3, 1024], P(None, 'groups'), parts along dimension 1, may hold values from -2 to 2
- exponents: float32 [1024], P('groups'), parts along dimension 0, may hold values from 0.2 to 1.5
- coefficients: float32 [1024], P('groups'), parts along dimension 0, may hold values from 0.5 to 2
Outputs:
- xc_matrix: float32 [1024, 512], P(('groups', 'blk', 'sub'), 'batch'), parts along dimension 0
The draws below stay inside these ranges and needn't reach their ends.
There are 2 independent parts, one for each index of `groups`. The reference program is written for one: setup_inputs(seed, part) draws one part's arguments, and reference() takes and returns one part's arrays. A program takes and returns all parts, laid end to end along the dimension named above; each array names one. Nothing has to cross between parts.
Inputs may be any that keep to these rules, and one draw needn't show every extreme that they name: A permutation: basis block b is row block block_home[b] of density and of xc_matrix; its owner is block_home[b] // 4. `significant`: each row lists 16 different basis blocks; among one row's blocks at most 4 have the same owner, and at least one owner holds exactly 4 of them. `density`: symmetric in basis order.
All inputs are finite; a program needn't handle non-finite values.
Results may differ from the reference program's by a relative error of at most 0.0029.
Values may be sent and summed in bfloat16 or wider, within the bound.
A program may use at most 64 MiB of HBM per device.

```python
import math
import jax
import jax.numpy as jnp
from jax import lax

BLOCK = 32
SIGBLK = 16
OWNBLK = 4
BATCH_PTS = 512
BATCHES = 2
SIGFN = 512
NBLOCKS = 16
NBASIS = 512
CAP = 4
WORKERS = 16
POINTS = 1024
N_BLK = 2
N_SUB = 2


def home_order(key):
    return jax.random.permutation(jax.random.fold_in(key, 101), NBLOCKS).astype(jnp.int32)


def draw_block_home(key, part):
    return home_order(key)


def draw_significant(key, part):
    order = home_order(key)
    key = jax.random.fold_in(key, 3)
    inverse = jnp.argsort(order, stable=True)
    owners = N_BLK * N_SUB
    pairs = jnp.arange(owners * CAP)
    pair_owner = pairs // CAP
    pair_copy = pairs % CAP

    def one_worker(worker_key):
        parts_keys = jax.random.split(worker_key, 4)
        forced = jax.random.randint(parts_keys[0], (), 0, owners)
        score = jax.random.permutation(parts_keys[1], owners * CAP).astype(jnp.int32) + 1
        score = jnp.where(pair_owner == forced, pair_copy - CAP, score)
        picked = jnp.argsort(score, stable=True)[:SIGBLK]
        shuffles = jax.vmap(lambda sub_key: jax.random.permutation(sub_key, OWNBLK))(jax.random.split(parts_keys[2], owners))
        local_index = shuffles[pair_owner[picked], pair_copy[picked]]
        chosen_blocks = inverse[pair_owner[picked] * OWNBLK + local_index]
        mixing = jax.random.permutation(parts_keys[3], SIGBLK)
        return chosen_blocks[mixing]
    return jax.vmap(one_worker)(jax.random.split(key, WORKERS)).astype(jnp.int32)


def draw_density(key, part):
    order = home_order(key)
    key = jax.random.fold_in(key, 5)
    raw = jax.random.normal(key, (NBASIS, NBASIS), jnp.float32)
    symmetric = (raw + raw.T) * (0.7071068 / math.sqrt(SIGFN))
    inverse = jnp.argsort(order, stable=True)
    arranged = symmetric.reshape(NBLOCKS, BLOCK, NBASIS)[inverse].reshape(NBASIS, NBASIS)
    return arranged.astype(jnp.bfloat16)


def level_of(stream_key, extent, shards, low, largest):
    factor_of, own = 1.0, jax.random.fold_in(stream_key, 6)
    for dim, blocks in shards:
        steps = jnp.exp(jax.random.uniform(jax.random.fold_in(own, dim), (blocks,), jnp.float32, low / len(shards), largest / len(shards)))
        factor_of = factor_of * jnp.repeat(steps, extent[dim] // blocks).reshape([-1 if axis == dim else 1 for axis in range(len(extent))])
    return factor_of


def setup_inputs(seed: int = 0, part: int = 0) -> dict:
    streams_of = jax.random.split(jax.random.key(seed), 9)
    own_keys = jax.random.split(jax.random.fold_in(streams_of[8], part), 9)
    density = draw_density(jax.random.fold_in(jax.random.fold_in(streams_of[8], part), 71), part)
    block_home = draw_block_home(jax.random.fold_in(jax.random.fold_in(streams_of[8], part), 71), part)
    significant = draw_significant(jax.random.fold_in(jax.random.fold_in(streams_of[8], part), 71), part)
    points = jnp.clip(jax.random.uniform(own_keys[3], (3, WORKERS * POINTS), jnp.float32, -2.0, 2.0) * level_of(own_keys[3], (3, WORKERS * POINTS), ((1, 16),), -0.4, 0.0), -2.0, 2.0)
    weights = jnp.clip(jnp.exp(math.log(0.0048828125) - 2.3025851 * jax.random.uniform(own_keys[4], (WORKERS * POINTS,), jnp.float32) ** level_of(own_keys[4], (WORKERS * POINTS,), ((0, 16),), -0.2, 0.2)), 0.00048828125, 0.0048828125)
    centers = jnp.clip(jax.random.uniform(own_keys[5], (3, NBASIS), jnp.float32, -2.0, 2.0), -2.0, 2.0)
    exponents = jnp.clip(jnp.exp(jax.random.uniform(own_keys[6], (NBASIS,), jnp.float32, math.log(0.2), math.log(1.5))), 0.2, 1.5)
    coefficients = jnp.clip(jnp.exp(jax.random.uniform(own_keys[7], (NBASIS,), jnp.float32, math.log(0.5), math.log(2.0))), 0.5, 2.0)
    return {"density": density, "block_home": block_home, "significant": significant, "points": points, "weights": weights, "centers": centers, "exponents": exponents, "coefficients": coefficients}


SLATER = 0.7386
KAPPA = 0.804
MU_PBE = 0.2195

def energy(charge, squares):
    scaled = jnp.sqrt(charge * charge + 1.0)
    gradient_ratio = squares / scaled ** (8.0 / 3.0)
    enhance = 1.0 + KAPPA - KAPPA / (1.0 + MU_PBE * gradient_ratio / KAPPA)
    return -SLATER * scaled ** (4.0 / 3.0) * enhance

def potentials(charge, squares):
    return jax.grad(lambda first_arg, second_arg: jnp.sum(energy(first_arg, second_arg)), argnums=(0, 1))(charge, squares)

def batch_moment(batch_points, batch_weights, center, exponent, coefficient, local_density):
    offset = batch_points[:, :, None] - center[:, None, :]
    distance = lax.optimization_barrier(jnp.sum(offset * offset, axis=0))
    value = coefficient[None, :] * jnp.exp(-exponent[None, :] * distance)
    basis = value.astype(jnp.bfloat16)
    slope = (-2.0 * exponent[None, None, :] * offset * value[None]).astype(jnp.bfloat16)
    mixed = jnp.dot(basis, local_density, preferred_element_type=jnp.float32)
    density_value = lax.optimization_barrier(jnp.sum(basis.astype(jnp.float32) * mixed, axis=1))
    grad_density = 2.0 * lax.optimization_barrier(jnp.sum(slope.astype(jnp.float32) * mixed[None], axis=2))
    gradient_sq = lax.optimization_barrier(jnp.sum(grad_density * grad_density, axis=0))
    pot_density, pot_gradient = potentials(density_value, gradient_sq)
    along = lax.optimization_barrier(jnp.sum(grad_density[:, :, None] * slope.astype(jnp.float32), axis=0))
    zeta = (batch_weights[:, None] * (0.5 * pot_density[:, None] * basis.astype(jnp.float32) + 2.0 * pot_gradient[:, None] * along)).astype(jnp.bfloat16)
    return lax.dot_general(basis, zeta, (((0,), (0,)), ((), ())), preferred_element_type=jnp.float32)

def reference(density, block_home, significant, points, weights, centers, exponents, coefficients):
    blocks = block_home.shape[0]
    block_width = density.shape[0] // blocks
    density_tiles = density.reshape(blocks, block_width, blocks, block_width)
    worker_points = points.reshape(3, WORKERS, POINTS).transpose(1, 0, 2)
    worker_weights = weights.reshape(WORKERS, POINTS)
    center_blocks = centers.reshape(3, blocks, block_width)
    exponent_blocks = exponents.reshape(blocks, block_width)
    coefficient_blocks = coefficients.reshape(blocks, block_width)

    def accumulate(running, worker_item):
        chosen, own_points, own_weights = worker_item
        stored_rows = block_home[chosen]
        local_density = density_tiles[stored_rows][:, :, chosen, :].reshape(SIGFN, SIGFN)
        center = center_blocks[:, chosen, :].reshape(3, SIGFN)
        exponent = exponent_blocks[chosen].reshape(SIGFN)
        coefficient = coefficient_blocks[chosen].reshape(SIGFN)
        moment = jnp.zeros((SIGFN, SIGFN), jnp.float32)
        for batch_index in range(BATCHES):
            first_point = batch_index * BATCH_PTS
            moment = moment + batch_moment(own_points[:, first_point:first_point + BATCH_PTS], own_weights[first_point:first_point + BATCH_PTS], center, exponent, coefficient, local_density)
        rounded = lax.optimization_barrier((moment + moment.T).astype(jnp.bfloat16))
        placed = rounded.astype(jnp.float32).reshape(SIGBLK, block_width, SIGBLK, block_width).transpose(0, 2, 1, 3)
        running = running.at[stored_rows[:, None], :, chosen[None, :], :].add(placed)
        return (running, None)
    start_value = jnp.zeros((blocks, block_width, blocks, block_width), jnp.float32)
    running, unused = lax.scan(accumulate, start_value, (significant, worker_points, worker_weights))
    return running.reshape(blocks * block_width, blocks * block_width)
```

```python
import jax
import jax.numpy as jnp
from jax import lax
from jax.experimental import pallas as pl
from jax.experimental.pallas import tpu as pltpu
from jax.sharding import PartitionSpec as P

BATCHES = 2


SLATER = 0.7386
KAPPA = 0.804
MU_PBE = 0.2195


def energy(charge, squares):
    scaled = jnp.sqrt(charge * charge + 1.0)
    gradient_ratio = squares / scaled ** (8.0 / 3.0)
    enhance = 1.0 + KAPPA - KAPPA / (1.0 + MU_PBE * gradient_ratio / KAPPA)
    return -SLATER * scaled ** (4.0 / 3.0) * enhance


def potentials(charge, squares):
    return jax.grad(
        lambda first_arg, second_arg: jnp.sum(energy(first_arg, second_arg)), argnums=(0, 1)
    )(charge, squares)


def batch_moment(batch_points, batch_weights, center, exponent, coefficient, local_density):
    offsets = [batch_points[comp][:, None] - center[comp][None, :] for comp in range(3)]
    distance = offsets[0] * offsets[0] + offsets[1] * offsets[1] + offsets[2] * offsets[2]
    value = coefficient[None, :] * jnp.exp(-exponent[None, :] * distance)
    basis = value.astype(jnp.bfloat16)
    slopes = [
        (-2.0 * exponent[None, :] * offsets[comp] * value).astype(jnp.bfloat16) for comp in range(3)
    ]
    mixed = jnp.dot(basis, local_density, preferred_element_type=jnp.float32)
    density_value = jnp.sum(basis.astype(jnp.float32) * mixed, axis=1)
    grads = [2.0 * jnp.sum(slopes[comp].astype(jnp.float32) * mixed, axis=1) for comp in range(3)]
    gradient_sq = grads[0] * grads[0] + grads[1] * grads[1] + grads[2] * grads[2]
    pot_density, pot_gradient = potentials(density_value, gradient_sq)
    along = grads[0][:, None] * slopes[0].astype(jnp.float32)
    along = along + grads[1][:, None] * slopes[1].astype(jnp.float32)
    along = along + grads[2][:, None] * slopes[2].astype(jnp.float32)
    zeta = (
        batch_weights[:, None]
        * (
            0.5 * pot_density[:, None] * basis.astype(jnp.float32)
            + 2.0 * pot_gradient[:, None] * along
        )
    ).astype(jnp.bfloat16)
    return lax.dot_general(
        basis, zeta, (((0,), (0,)), ((), ())), preferred_element_type=jnp.float32
    )


def body(density, block_home, significant, points, weights, centers, exponents, coefficients):
    owners = lax.axis_size(("blk", "sub"))
    blocks = block_home.shape[0]
    block_width = density.shape[1] // blocks
    held = density.shape[0] // block_width
    listed = significant.shape[1]
    capacity = min(held, max(2, 2 * listed // owners))
    chosen = significant[0]
    position = block_home[chosen]
    owner_of = position // held
    local_of = position % held
    ordinal = jnp.arange(listed)
    earlier = ordinal[None, :] < ordinal[:, None]
    rank_of = jnp.sum((owner_of[None, :] == owner_of[:, None]) & earlier, axis=1)
    slot_of = owner_of * capacity + rank_of
    slot_hit = slot_of[None, :] == jnp.arange(owners * capacity)[:, None]
    asked = jnp.sum(jnp.where(slot_hit, local_of[None, :] + 1, 0), axis=1) - 1
    message = jnp.concatenate(
        [asked.reshape(owners, capacity), jnp.broadcast_to(chosen[None, :], (owners, listed))],
        axis=1,
    )
    received = lax.all_to_all(message, ("blk", "sub"), split_axis=0, concat_axis=0, tiled=True)
    wanted = received[:, :capacity]
    their_lists = received[:, capacity:]
    density_tiles = density.reshape(held, block_width, blocks, block_width)

    def pick(columns, rows_wanted):
        column_cut = jnp.take(density_tiles, columns, axis=2)
        taken = jnp.take(column_cut, jnp.maximum(rows_wanted, 0), axis=0)
        taken = jnp.where((rows_wanted >= 0)[:, None, None, None], taken, jnp.zeros_like(taken))
        return taken.reshape(capacity, block_width, listed * block_width)

    reply = jax.vmap(pick)(their_lists, wanted)
    fetched = lax.all_to_all(reply, ("blk", "sub"), split_axis=0, concat_axis=0, tiled=True)
    slots_flat = fetched.reshape(owners * capacity, block_width, listed * block_width)
    local_density = jnp.take(slots_flat, slot_of, axis=0).reshape(
        listed * block_width, listed * block_width
    )
    center = centers.reshape(3, blocks, block_width)[:, chosen, :].reshape(3, listed * block_width)
    exponent = exponents.reshape(blocks, block_width)[chosen].reshape(listed * block_width)
    coefficient = coefficients.reshape(blocks, block_width)[chosen].reshape(listed * block_width)
    batch_points = points.shape[1] // BATCHES
    moment = jnp.zeros((listed * block_width, listed * block_width), jnp.float32)
    for batch_index in range(BATCHES):
        first_point = batch_index * batch_points
        moment = moment + batch_moment(
            points[:, first_point : first_point + batch_points],
            weights[first_point : first_point + batch_points],
            center,
            exponent,
            coefficient,
            local_density,
        )
    partial_rows = (
        (moment + moment.T).astype(jnp.bfloat16).reshape(listed, block_width, listed * block_width)
    )
    entry_of = jnp.sum(jnp.where(slot_hit, ordinal[None, :] + 1, 0), axis=1) - 1
    outgoing = jnp.take(partial_rows, jnp.maximum(entry_of, 0), axis=0)
    outgoing = jnp.where((entry_of >= 0)[:, None, None], outgoing, jnp.zeros_like(outgoing))
    outgoing = outgoing.reshape(owners, capacity, block_width, listed * block_width)
    returned = lax.all_to_all(outgoing, ("blk", "sub"), split_axis=0, concat_axis=0, tiled=True)
    row_hot = (wanted[:, :, None] == jnp.arange(held)[None, None, :]).astype(jnp.bfloat16)
    grouped = jnp.einsum(
        "scl,scikj->slikj",
        row_hot,
        returned.reshape(owners, capacity, block_width, listed, block_width),
        preferred_element_type=jnp.float32,
    ).astype(jnp.bfloat16)
    column_hot = (their_lists[:, :, None] == jnp.arange(blocks)[None, None, :]).astype(jnp.bfloat16)
    summed = jnp.einsum("skn,slikj->linj", column_hot, grouped, preferred_element_type=jnp.float32)
    return lax.psum_scatter(
        summed.reshape(held * block_width, blocks * block_width),
        "batch",
        scatter_dimension=1,
        tiled=True,
    )


LOG2E = 1.4426950408889634
PAIRS = ((0, 0), (0, 1), (1, 0), (0, 2), (1, 1), (2, 0))
SINGLES = (0, 2, 5)
TERMS = 5


def three_parts(value):
    first = value.astype(jnp.bfloat16).astype(jnp.float32)
    rest = value - first
    second = rest.astype(jnp.bfloat16).astype(jnp.float32)
    third = (rest - second).astype(jnp.bfloat16).astype(jnp.float32)
    return first, second, third


def fill_rows(ref, base, rows, side):
    for term, row in enumerate(rows):
        parts = three_parts(row)
        for place, pair in enumerate(PAIRS):
            index = base + term * len(PAIRS) + place
            ref[index : index + 1, :] = parts[pair[side]]
    last = base + TERMS * len(PAIRS)
    ref[last : base + 32, :] = jnp.zeros((base + 32 - last, ref.shape[1]), jnp.float32)


def nt_dot(left, right):
    return lax.dot_general(
        left, right, (((1,), (1,)), ((), ())), preferred_element_type=jnp.float32
    )


def dense_kernel(
    home_ref, density_ref, points_ref, weights_ref, centers_ref, exponents_ref, coefficients_ref,
    out_ref,
    place_hot, param_rows, point_rows, arg_cols, pot_cols, pot_rows,
    own_density, gathered, basis, zeta, sums, near, give_core, take_core, give_chip, take_chip,
    give_batch, take_batch,
    gather_send, gather_recv, core_send, core_recv, chip_send, chip_recv, batch_send, batch_recv,
):
    blk, sub, batch = lax.axis_index("blk"), lax.axis_index("sub"), lax.axis_index("batch")
    rows, functions = density_ref.shape
    blocks = home_ref.shape[0]
    width = functions // blocks
    count = points_ref.shape[1]
    columns = out_ref.shape[1]
    core_peer = {"sub": 1 - sub}
    chip_peer = {"blk": 1 - blk}
    chunk_of = [3 - batch, (batch + 2) % 4, batch + 1 - 2 * (batch % 2), batch]
    batch_peers = [{"batch": chunk_of[k]} for k in range(3)]

    barrier = pltpu.get_barrier_semaphore()
    for peer in [core_peer, chip_peer] + batch_peers:
        pl.semaphore_signal(barrier, inc=1, device_id=peer, device_id_type=pl.DeviceIdType.MESH)

    gap = lax.broadcasted_iota(jnp.int32, (width, functions), 1) - lax.broadcasted_iota(
        jnp.int32, (width, functions), 0
    )
    for index in range(blocks):
        place_hot[index * width : (index + 1) * width, :] = jnp.where(
            gap == home_ref[index] * width, 1.0, 0.0
        ).astype(jnp.bfloat16)
    own_density[...] = jnp.dot(
        density_ref[...], place_hot[...], preferred_element_type=jnp.float32
    ).astype(jnp.bfloat16)

    pl.semaphore_wait(barrier, 5)

    def remote(source, target, send, recv, peer):
        return pltpu.make_async_remote_copy(
            src_ref=source, dst_ref=target, send_sem=send, recv_sem=recv,
            device_id=peer, device_id_type=pl.DeviceIdType.MESH,
        )

    to_chip = remote(own_density, gathered.at[1], gather_send.at[1], gather_recv.at[1], chip_peer)
    to_core = remote(own_density, gathered.at[0], gather_send.at[0], gather_recv.at[0], core_peer)
    forward = remote(gathered.at[1], gathered.at[2], gather_send.at[2], gather_recv.at[2], core_peer)
    to_chip.start()
    to_core.start()

    exponent = exponents_ref[...]
    center = [centers_ref[comp : comp + 1, :] for comp in range(3)]
    point = [points_ref[comp : comp + 1, :] for comp in range(3)]
    scaled = exponent * LOG2E
    norm = center[0] * center[0] + center[1] * center[1] + center[2] * center[2]
    constant = jnp.log(coefficients_ref[...]) * LOG2E - scaled * norm
    fill_rows(
        param_rows, 0, [constant] + [2.0 * scaled * center[comp] for comp in range(3)] + [-scaled], 0
    )
    fill_rows(
        param_rows, 32,
        [jnp.ones_like(exponent), exponent] + [exponent * center[comp] for comp in range(3)], 0,
    )
    radius = point[0] * point[0] + point[1] * point[1] + point[2] * point[2]
    fill_rows(point_rows, 0, [jnp.ones_like(radius)] + point + [radius], 1)
    placed = jnp.dot(
        param_rows[...].astype(jnp.bfloat16), place_hot[...], preferred_element_type=jnp.float32
    )
    arg_cols[...] = jnp.transpose(placed[0:32, :]).astype(jnp.bfloat16)
    pot_cols[...] = jnp.transpose(placed[32:64, :]).astype(jnp.bfloat16)
    pot_rows[...] = placed[32:64, :].astype(jnp.bfloat16)

    piece = 512
    point_parts = point_rows[...].astype(jnp.bfloat16)
    for row in range(0, functions, rows):
        for column in range(0, count, piece):
            argument = jnp.dot(
                arg_cols[row : row + rows, :], point_parts[:, column : column + piece],
                preferred_element_type=jnp.float32,
            )
            basis[row : row + rows, column : column + piece] = jnp.exp2(argument).astype(
                jnp.bfloat16
            )

    def owner_rows(owner):
        return pl.ds(pl.multiple_of(owner * rows, rows), rows)

    def accumulate(stage, held_rows, owner):
        own = pot_rows[:, owner_rows(owner)]
        for column in range(0, count, piece):
            mixed = jnp.dot(
                held_rows, basis[:, column : column + piece], preferred_element_type=jnp.float32
            )
            value = basis[owner_rows(owner), column : column + piece].astype(jnp.float32)
            total = jnp.dot(
                own, (mixed * value).astype(jnp.bfloat16), preferred_element_type=jnp.float32
            )
            if stage > 0:
                total = total + sums[:, column : column + piece]
            sums[:, column : column + piece] = total

    accumulate(0, own_density[...], blk * 2 + sub)
    to_core.wait_recv()
    accumulate(1, gathered[0], blk * 2 + 1 - sub)
    to_chip.wait_recv()
    forward.start()
    accumulate(2, gathered[1], (1 - blk) * 2 + sub)
    forward.wait_recv()
    accumulate(3, gathered[2], (1 - blk) * 2 + 1 - sub)

    moments = []
    for term in range(TERMS):
        base = term * len(PAIRS)
        moment = sums[base : base + 1, :]
        for place in SINGLES[1:]:
            moment = moment + sums[base + place : base + place + 1, :]
        moments.append(moment)
    charge = moments[0]
    grads = [-4.0 * (point[comp] * moments[1] - moments[2 + comp]) for comp in range(3)]
    squares = grads[0] * grads[0] + grads[1] * grads[1] + grads[2] * grads[2]
    shrink = jnp.exp(jnp.log(charge * charge + 1.0) * (-1.0 / 3.0))
    shrink_sq = shrink * shrink
    ratio = squares * shrink_sq * shrink_sq
    inner = 1.0 / (1.0 + (MU_PBE / KAPPA) * ratio)
    enhance = 1.0 + KAPPA - KAPPA * inner
    slope = MU_PBE * ratio * inner * inner
    pot_density = -SLATER * charge * shrink * ((4.0 / 3.0) * enhance - (8.0 / 3.0) * slope)
    pot_gradient = -SLATER * MU_PBE * shrink_sq * inner * inner
    weight = weights_ref[...]
    lean = [4.0 * weight * pot_gradient * grads[comp] for comp in range(3)]
    along = -(lean[0] * point[0] + lean[1] * point[1] + lean[2] * point[2])
    fill_rows(point_rows, 0, [0.5 * weight * pot_density, along] + lean, 1)
    pot_parts = point_rows[...].astype(jnp.bfloat16)
    for row in range(0, functions, rows):
        for column in range(0, count, piece):
            factor = jnp.dot(
                pot_cols[row : row + rows, :], pot_parts[:, column : column + piece],
                preferred_element_type=jnp.float32,
            )
            value = basis[row : row + rows, column : column + piece].astype(jnp.float32)
            zeta[row : row + rows, column : column + piece] = (value * factor).astype(jnp.bfloat16)

    def partial_rows(owner):
        held_rows = owner_rows(owner)
        product = nt_dot(basis[held_rows, :], zeta[...]) + nt_dot(zeta[held_rows, :], basis[...])
        return nt_dot(product.astype(jnp.bfloat16), place_hot[...])

    core_copies, chip_copies, batch_copies = [], [], []
    for turn in range(2):
        give_core[turn] = partial_rows(
            (1 - blk if turn == 0 else blk) * 2 + 1 - sub
        ).astype(jnp.bfloat16)
        copy = remote(
            give_core.at[turn], take_core.at[turn], core_send.at[turn], core_recv.at[turn], core_peer
        )
        copy.start()
        core_copies.append(copy)
    near[...] = partial_rows((1 - blk) * 2 + sub)
    core_copies[0].wait_recv()
    for chunk in range(4):
        lanes = pl.ds(pl.multiple_of(chunk_of[chunk] * columns, columns), columns)
        give_chip[chunk] = (near[:, lanes] + take_core[0, :, lanes].astype(jnp.float32)).astype(
            jnp.bfloat16
        )
        copy = remote(
            give_chip.at[chunk], take_chip.at[chunk], chip_send.at[chunk], chip_recv.at[chunk],
            chip_peer,
        )
        copy.start()
        chip_copies.append(copy)
    near[...] = partial_rows(blk * 2 + sub)
    core_copies[1].wait_recv()
    for chunk in range(4):
        lanes = pl.ds(pl.multiple_of(chunk_of[chunk] * columns, columns), columns)
        total = near[:, lanes] + take_core[1, :, lanes].astype(jnp.float32)
        chip_copies[chunk].wait_recv()
        total = total + take_chip[chunk].astype(jnp.float32)
        if chunk < 3:
            give_batch[chunk] = total.astype(jnp.bfloat16)
            copy = remote(
                give_batch.at[chunk], take_batch.at[chunk], batch_send.at[chunk],
                batch_recv.at[chunk], batch_peers[chunk],
            )
            copy.start()
            batch_copies.append(copy)
    for chunk in (2, 1, 0):
        batch_copies[chunk].wait_recv()
        total = total + take_batch[chunk].astype(jnp.float32)
    out_ref[...] = total
    for copy in [to_chip, to_core, forward] + core_copies + chip_copies + batch_copies:
        copy.wait_send()


def dense_body(density, block_home, significant, points, weights, centers, exponents, coefficients):
    rows, functions = density.shape
    count = points.shape[1]
    columns = functions // 4
    f32, bf16 = jnp.float32, jnp.bfloat16
    vmem = pl.BlockSpec(memory_space=pltpu.VMEM)
    return pl.pallas_call(
        dense_kernel,
        out_shape=jax.ShapeDtypeStruct((rows, columns), f32),
        in_specs=[pl.BlockSpec(memory_space=pltpu.SMEM)] + [vmem] * 6,
        out_specs=vmem,
        scratch_shapes=[
            pltpu.VMEM((functions, functions), bf16),
            pltpu.VMEM((64, functions), f32),
            pltpu.VMEM((32, count), f32),
            pltpu.VMEM((functions, 32), bf16),
            pltpu.VMEM((functions, 32), bf16),
            pltpu.VMEM((32, functions), bf16),
            pltpu.VMEM((rows, functions), bf16),
            pltpu.VMEM((3, rows, functions), bf16),
            pltpu.VMEM((functions, count), bf16),
            pltpu.VMEM((functions, count), bf16),
            pltpu.VMEM((32, count), f32),
            pltpu.VMEM((rows, functions), f32),
            pltpu.VMEM((2, rows, functions), bf16),
            pltpu.VMEM((2, rows, functions), bf16),
            pltpu.VMEM((4, rows, columns), bf16),
            pltpu.VMEM((4, rows, columns), bf16),
            pltpu.VMEM((3, rows, columns), bf16),
            pltpu.VMEM((3, rows, columns), bf16),
        ]
        + [pltpu.SemaphoreType.DMA((size,)) for size in (3, 3, 2, 2, 4, 4, 3, 3)],
        compiler_params=pltpu.CompilerParams(
            collective_id=0, has_side_effects=True, vmem_limit_bytes=48 * 1024 * 1024
        ),
    )(
        block_home, density, points, weights.reshape(1, count), centers,
        exponents.reshape(1, functions), coefficients.reshape(1, functions),
    )


def every_block_listed(mesh, density, block_home, significant):
    shape = dict(mesh.shape)
    return (
        significant.shape[1] == block_home.shape[0] // shape["groups"]
        and (shape["blk"], shape["sub"], shape["batch"]) == (2, 2, 4)
    )


def solution(mesh):
    def whole(density, block_home, significant, *others):
        dense = every_block_listed(mesh, density, block_home, significant)
        return jax.shard_map(
            dense_body if dense else body,
            mesh=mesh,
            in_specs=(
                P(("groups", "blk", "sub"), None),
                P("groups"),
                P(("groups", "batch", "blk", "sub"), None),
                P(None, ("groups", "batch", "blk", "sub")),
                P(("groups", "batch", "blk", "sub")),
                P(None, "groups"),
                P("groups"),
                P("groups"),
            ),
            out_specs=P(("groups", "blk", "sub"), "batch"),
            check_vma=False,
        )(density, block_home, significant, *others)

    return whole
```

```python
import jax
import jax.numpy as jnp
from jax import lax
from jax.experimental import pallas as pl
from jax.experimental.pallas import tpu as pltpu
from jax.sharding import PartitionSpec as P

BATCHES = 2


SLATER = 0.7386
KAPPA = 0.804
MU_PBE = 0.2195


def energy(charge, squares):
    scaled = jnp.sqrt(charge * charge + 1.0)
    gradient_ratio = squares / scaled ** (8.0 / 3.0)
    enhance = 1.0 + KAPPA - KAPPA / (1.0 + MU_PBE * gradient_ratio / KAPPA)
    return -SLATER * scaled ** (4.0 / 3.0) * enhance


def potentials(charge, squares):
    return jax.grad(
        lambda first_arg, second_arg: jnp.sum(energy(first_arg, second_arg)), argnums=(0, 1)
    )(charge, squares)


def batch_moment(batch_points, batch_weights, center, exponent, coefficient, local_density):
    offsets = [batch_points[comp][:, None] - center[comp][None, :] for comp in range(3)]
    distance = offsets[0] * offsets[0] + offsets[1] * offsets[1] + offsets[2] * offsets[2]
    value = coefficient[None, :] * jnp.exp(-exponent[None, :] * distance)
    basis = value.astype(jnp.bfloat16)
    slopes = [
        (-2.0 * exponent[None, :] * offsets[comp] * value).astype(jnp.bfloat16) for comp in range(3)
    ]
    mixed = jnp.dot(basis, local_density, preferred_element_type=jnp.float32)
    density_value = jnp.sum(basis.astype(jnp.float32) * mixed, axis=1)
    grads = [2.0 * jnp.sum(slopes[comp].astype(jnp.float32) * mixed, axis=1) for comp in range(3)]
    gradient_sq = grads[0] * grads[0] + grads[1] * grads[1] + grads[2] * grads[2]
    pot_density, pot_gradient = potentials(density_value, gradient_sq)
    along = grads[0][:, None] * slopes[0].astype(jnp.float32)
    along = along + grads[1][:, None] * slopes[1].astype(jnp.float32)
    along = along + grads[2][:, None] * slopes[2].astype(jnp.float32)
    zeta = (
        batch_weights[:, None]
        * (
            0.5 * pot_density[:, None] * basis.astype(jnp.float32)
            + 2.0 * pot_gradient[:, None] * along
        )
    ).astype(jnp.bfloat16)
    return lax.dot_general(
        basis, zeta, (((0,), (0,)), ((), ())), preferred_element_type=jnp.float32
    )


def body(density, block_home, significant, points, weights, centers, exponents, coefficients):
    owners = lax.axis_size(("blk", "sub"))
    blocks = block_home.shape[0]
    block_width = density.shape[1] // blocks
    held = density.shape[0] // block_width
    listed = significant.shape[1]
    capacity = min(held, max(2, 2 * listed // owners))
    chosen = significant[0]
    position = block_home[chosen]
    owner_of = position // held
    local_of = position % held
    ordinal = jnp.arange(listed)
    earlier = ordinal[None, :] < ordinal[:, None]
    rank_of = jnp.sum((owner_of[None, :] == owner_of[:, None]) & earlier, axis=1)
    slot_of = owner_of * capacity + rank_of
    slot_hit = slot_of[None, :] == jnp.arange(owners * capacity)[:, None]
    asked = jnp.sum(jnp.where(slot_hit, local_of[None, :] + 1, 0), axis=1) - 1
    message = jnp.concatenate(
        [asked.reshape(owners, capacity), jnp.broadcast_to(chosen[None, :], (owners, listed))],
        axis=1,
    )
    received = lax.all_to_all(message, ("blk", "sub"), split_axis=0, concat_axis=0, tiled=True)
    wanted = received[:, :capacity]
    their_lists = received[:, capacity:]
    density_tiles = density.reshape(held, block_width, blocks, block_width)

    def pick(columns, rows_wanted):
        column_cut = jnp.take(density_tiles, columns, axis=2)
        taken = jnp.take(column_cut, jnp.maximum(rows_wanted, 0), axis=0)
        taken = jnp.where((rows_wanted >= 0)[:, None, None, None], taken, jnp.zeros_like(taken))
        return taken.reshape(capacity, block_width, listed * block_width)

    reply = jax.vmap(pick)(their_lists, wanted)
    fetched = lax.all_to_all(reply, ("blk", "sub"), split_axis=0, concat_axis=0, tiled=True)
    slots_flat = fetched.reshape(owners * capacity, block_width, listed * block_width)
    local_density = jnp.take(slots_flat, slot_of, axis=0).reshape(
        listed * block_width, listed * block_width
    )
    center = centers.reshape(3, blocks, block_width)[:, chosen, :].reshape(3, listed * block_width)
    exponent = exponents.reshape(blocks, block_width)[chosen].reshape(listed * block_width)
    coefficient = coefficients.reshape(blocks, block_width)[chosen].reshape(listed * block_width)
    batch_points = points.shape[1] // BATCHES
    moment = jnp.zeros((listed * block_width, listed * block_width), jnp.float32)
    for batch_index in range(BATCHES):
        first_point = batch_index * batch_points
        moment = moment + batch_moment(
            points[:, first_point : first_point + batch_points],
            weights[first_point : first_point + batch_points],
            center,
            exponent,
            coefficient,
            local_density,
        )
    partial_rows = (
        (moment + moment.T).astype(jnp.bfloat16).reshape(listed, block_width, listed * block_width)
    )
    entry_of = jnp.sum(jnp.where(slot_hit, ordinal[None, :] + 1, 0), axis=1) - 1
    outgoing = jnp.take(partial_rows, jnp.maximum(entry_of, 0), axis=0)
    outgoing = jnp.where((entry_of >= 0)[:, None, None], outgoing, jnp.zeros_like(outgoing))
    outgoing = outgoing.reshape(owners, capacity, block_width, listed * block_width)
    returned = lax.all_to_all(outgoing, ("blk", "sub"), split_axis=0, concat_axis=0, tiled=True)
    row_hot = (wanted[:, :, None] == jnp.arange(held)[None, None, :]).astype(jnp.bfloat16)
    grouped = jnp.einsum(
        "scl,scikj->slikj",
        row_hot,
        returned.reshape(owners, capacity, block_width, listed, block_width),
        preferred_element_type=jnp.float32,
    ).astype(jnp.bfloat16)
    column_hot = (their_lists[:, :, None] == jnp.arange(blocks)[None, None, :]).astype(jnp.bfloat16)
    summed = jnp.einsum("skn,slikj->linj", column_hot, grouped, preferred_element_type=jnp.float32)
    return lax.psum_scatter(
        summed.reshape(held * block_width, blocks * block_width),
        "batch",
        scatter_dimension=1,
        tiled=True,
    )


LOG2E = 1.4426950408889634
PAIRS = ((0, 0), (0, 1), (1, 0), (0, 2), (1, 1), (2, 0))
SINGLES = (0, 2, 5)
TERMS = 5


def three_parts(value):
    first = value.astype(jnp.bfloat16).astype(jnp.float32)
    rest = value - first
    second = rest.astype(jnp.bfloat16).astype(jnp.float32)
    third = (rest - second).astype(jnp.bfloat16).astype(jnp.float32)
    return first, second, third


def fill_rows(ref, base, rows, side):
    for term, row in enumerate(rows):
        parts = three_parts(row)
        for place, pair in enumerate(PAIRS):
            index = base + term * len(PAIRS) + place
            ref[index : index + 1, :] = parts[pair[side]]
    last = base + TERMS * len(PAIRS)
    ref[last : base + 32, :] = jnp.zeros((base + 32 - last, ref.shape[1]), jnp.float32)


def nt_dot(left, right):
    return lax.dot_general(
        left, right, (((1,), (1,)), ((), ())), preferred_element_type=jnp.float32
    )


def dense_kernel(
    home_in, density_in, points_in, weights_in, centers_in, exponents_in, coefficients_in,
    out_ref,
    home_ref, density_ref, points_ref, weights_ref, centers_ref, exponents_ref, coefficients_ref,
    place_hot, param_rows, point_rows, arg_cols, pot_cols, pot_rows,
    own_density, gathered, basis, zeta, sums, near, give_core, take_core, give_chip, take_chip,
    give_batch, take_batch,
    load_done,
    gather_send, gather_recv, core_send, core_recv, chip_send, chip_recv, batch_send, batch_recv,
):
    blk, sub, batch = lax.axis_index("blk"), lax.axis_index("sub"), lax.axis_index("batch")
    rows, functions = density_ref.shape
    blocks = home_ref.shape[0]
    width = functions // blocks
    count = points_ref.shape[1]
    columns = out_ref.shape[1]
    core_peer = {"sub": 1 - sub}
    chip_peer = {"blk": 1 - blk}
    chunk_of = [3 - batch, (batch + 2) % 4, batch + 1 - 2 * (batch % 2), batch]
    batch_peers = [{"batch": chunk_of[k]} for k in range(3)]

    barrier = pltpu.get_barrier_semaphore()
    for peer in [core_peer, chip_peer] + batch_peers:
        pl.semaphore_signal(barrier, inc=1, device_id=peer, device_id_type=pl.DeviceIdType.MESH)

    loads = []
    for source, target in (
        (home_in, home_ref), (density_in, density_ref), (centers_in, centers_ref),
        (exponents_in, exponents_ref), (coefficients_in, coefficients_ref),
        (points_in, points_ref), (weights_in, weights_ref),
    ):
        copy = pltpu.make_async_copy(source, target, load_done.at[len(loads)])
        copy.start()
        loads.append(copy)

    gap = lax.broadcasted_iota(jnp.int32, (width, functions), 1) - lax.broadcasted_iota(
        jnp.int32, (width, functions), 0
    )
    loads[0].wait()
    for index in range(blocks):
        place_hot[index * width : (index + 1) * width, :] = jnp.where(
            gap == home_ref[index] * width, 1.0, 0.0
        ).astype(jnp.bfloat16)
    loads[1].wait()
    own_density[...] = jnp.dot(
        density_ref[...], place_hot[...], preferred_element_type=jnp.float32
    ).astype(jnp.bfloat16)

    pl.semaphore_wait(barrier, 5)

    def remote(source, target, send, recv, peer):
        return pltpu.make_async_remote_copy(
            src_ref=source, dst_ref=target, send_sem=send, recv_sem=recv,
            device_id=peer, device_id_type=pl.DeviceIdType.MESH,
        )

    to_chip = remote(own_density, gathered.at[1], gather_send.at[1], gather_recv.at[1], chip_peer)
    to_core = remote(own_density, gathered.at[0], gather_send.at[0], gather_recv.at[0], core_peer)
    forward = remote(gathered.at[1], gathered.at[2], gather_send.at[2], gather_recv.at[2], core_peer)
    to_chip.start()
    to_core.start()

    for copy in loads[2:]:
        copy.wait()
    exponent = exponents_ref[...]
    center = [centers_ref[comp : comp + 1, :] for comp in range(3)]
    point = [points_ref[comp : comp + 1, :] for comp in range(3)]
    scaled = exponent * LOG2E
    norm = center[0] * center[0] + center[1] * center[1] + center[2] * center[2]
    constant = jnp.log(coefficients_ref[...]) * LOG2E - scaled * norm
    fill_rows(
        param_rows, 0, [constant] + [2.0 * scaled * center[comp] for comp in range(3)] + [-scaled], 0
    )
    fill_rows(
        param_rows, 32,
        [jnp.ones_like(exponent), exponent] + [exponent * center[comp] for comp in range(3)], 0,
    )
    radius = point[0] * point[0] + point[1] * point[1] + point[2] * point[2]
    fill_rows(point_rows, 0, [jnp.ones_like(radius)] + point + [radius], 1)
    placed = jnp.dot(
        param_rows[...].astype(jnp.bfloat16), place_hot[...], preferred_element_type=jnp.float32
    )
    arg_cols[...] = jnp.transpose(placed[0:32, :]).astype(jnp.bfloat16)
    pot_cols[...] = jnp.transpose(placed[32:64, :]).astype(jnp.bfloat16)
    pot_rows[...] = placed[32:64, :].astype(jnp.bfloat16)

    piece = 512
    point_parts = point_rows[...].astype(jnp.bfloat16)
    for row in range(0, functions, rows):
        for column in range(0, count, piece):
            argument = jnp.dot(
                arg_cols[row : row + rows, :], point_parts[:, column : column + piece],
                preferred_element_type=jnp.float32,
            )
            basis[row : row + rows, column : column + piece] = jnp.exp2(argument).astype(
                jnp.bfloat16
            )

    def owner_rows(owner):
        return pl.ds(pl.multiple_of(owner * rows, rows), rows)

    def accumulate(stage, held_rows, owner):
        own = pot_rows[:, owner_rows(owner)]
        for column in range(0, count, piece):
            mixed = jnp.dot(
                held_rows, basis[:, column : column + piece], preferred_element_type=jnp.float32
            )
            value = basis[owner_rows(owner), column : column + piece].astype(jnp.float32)
            total = jnp.dot(
                own, (mixed * value).astype(jnp.bfloat16), preferred_element_type=jnp.float32
            )
            if stage > 0:
                total = total + sums[:, column : column + piece]
            sums[:, column : column + piece] = total

    accumulate(0, own_density[...], blk * 2 + sub)
    to_core.wait_recv()
    accumulate(1, gathered[0], blk * 2 + 1 - sub)
    to_chip.wait_recv()
    forward.start()
    accumulate(2, gathered[1], (1 - blk) * 2 + sub)
    forward.wait_recv()
    accumulate(3, gathered[2], (1 - blk) * 2 + 1 - sub)

    moments = []
    for term in range(TERMS):
        base = term * len(PAIRS)
        moment = sums[base : base + 1, :]
        for place in SINGLES[1:]:
            moment = moment + sums[base + place : base + place + 1, :]
        moments.append(moment)
    charge = moments[0]
    grads = [-4.0 * (point[comp] * moments[1] - moments[2 + comp]) for comp in range(3)]
    squares = grads[0] * grads[0] + grads[1] * grads[1] + grads[2] * grads[2]
    shrink = jnp.exp(jnp.log(charge * charge + 1.0) * (-1.0 / 3.0))
    shrink_sq = shrink * shrink
    ratio = squares * shrink_sq * shrink_sq
    inner = 1.0 / (1.0 + (MU_PBE / KAPPA) * ratio)
    enhance = 1.0 + KAPPA - KAPPA * inner
    slope = MU_PBE * ratio * inner * inner
    pot_density = -SLATER * charge * shrink * ((4.0 / 3.0) * enhance - (8.0 / 3.0) * slope)
    pot_gradient = -SLATER * MU_PBE * shrink_sq * inner * inner
    weight = weights_ref[...]
    lean = [4.0 * weight * pot_gradient * grads[comp] for comp in range(3)]
    along = -(lean[0] * point[0] + lean[1] * point[1] + lean[2] * point[2])
    fill_rows(point_rows, 0, [0.5 * weight * pot_density, along] + lean, 1)
    pot_parts = point_rows[...].astype(jnp.bfloat16)
    for row in range(0, functions, rows):
        for column in range(0, count, piece):
            factor = jnp.dot(
                pot_cols[row : row + rows, :], pot_parts[:, column : column + piece],
                preferred_element_type=jnp.float32,
            )
            value = basis[row : row + rows, column : column + piece].astype(jnp.float32)
            zeta[row : row + rows, column : column + piece] = (value * factor).astype(jnp.bfloat16)

    def partial_rows(owner):
        held_rows = owner_rows(owner)
        product = nt_dot(basis[held_rows, :], zeta[...]) + nt_dot(zeta[held_rows, :], basis[...])
        return nt_dot(product.astype(jnp.bfloat16), place_hot[...])

    core_copies, chip_copies, batch_copies = [], [], []
    for turn in range(2):
        give_core[turn] = partial_rows(
            (1 - blk if turn == 0 else blk) * 2 + 1 - sub
        ).astype(jnp.bfloat16)
        copy = remote(
            give_core.at[turn], take_core.at[turn], core_send.at[turn], core_recv.at[turn], core_peer
        )
        copy.start()
        core_copies.append(copy)
    near[...] = partial_rows((1 - blk) * 2 + sub)
    core_copies[0].wait_recv()
    for chunk in range(4):
        lanes = pl.ds(pl.multiple_of(chunk_of[chunk] * columns, columns), columns)
        give_chip[chunk] = (near[:, lanes] + take_core[0, :, lanes].astype(jnp.float32)).astype(
            jnp.bfloat16
        )
        copy = remote(
            give_chip.at[chunk], take_chip.at[chunk], chip_send.at[chunk], chip_recv.at[chunk],
            chip_peer,
        )
        copy.start()
        chip_copies.append(copy)
    near[...] = partial_rows(blk * 2 + sub)
    core_copies[1].wait_recv()
    for chunk in range(4):
        lanes = pl.ds(pl.multiple_of(chunk_of[chunk] * columns, columns), columns)
        total = near[:, lanes] + take_core[1, :, lanes].astype(jnp.float32)
        chip_copies[chunk].wait_recv()
        total = total + take_chip[chunk].astype(jnp.float32)
        if chunk < 3:
            give_batch[chunk] = total.astype(jnp.bfloat16)
            copy = remote(
                give_batch.at[chunk], take_batch.at[chunk], batch_send.at[chunk],
                batch_recv.at[chunk], batch_peers[chunk],
            )
            copy.start()
            batch_copies.append(copy)
    for chunk in (2, 1, 0):
        batch_copies[chunk].wait_recv()
        total = total + take_batch[chunk].astype(jnp.float32)
    out_ref[...] = total
    for copy in [to_chip, to_core, forward] + core_copies + chip_copies + batch_copies:
        copy.wait_send()


def dense_body(density, block_home, significant, points, weights, centers, exponents, coefficients):
    rows, functions = density.shape
    count = points.shape[1]
    columns = functions // 4
    f32, bf16 = jnp.float32, jnp.bfloat16
    vmem = pl.BlockSpec(memory_space=pltpu.VMEM)
    return pl.pallas_call(
        dense_kernel,
        out_shape=jax.ShapeDtypeStruct((rows, columns), f32),
        in_specs=[pl.BlockSpec(memory_space=pltpu.HBM)] * 7,
        out_specs=vmem,
        scratch_shapes=[
            pltpu.SMEM(block_home.shape, jnp.int32),
            pltpu.VMEM((rows, functions), bf16),
            pltpu.VMEM((3, count), f32),
            pltpu.VMEM((1, count), f32),
            pltpu.VMEM((3, functions), f32),
            pltpu.VMEM((1, functions), f32),
            pltpu.VMEM((1, functions), f32),
            pltpu.VMEM((functions, functions), bf16),
            pltpu.VMEM((64, functions), f32),
            pltpu.VMEM((32, count), f32),
            pltpu.VMEM((functions, 32), bf16),
            pltpu.VMEM((functions, 32), bf16),
            pltpu.VMEM((32, functions), bf16),
            pltpu.VMEM((rows, functions), bf16),
            pltpu.VMEM((3, rows, functions), bf16),
            pltpu.VMEM((functions, count), bf16),
            pltpu.VMEM((functions, count), bf16),
            pltpu.VMEM((32, count), f32),
            pltpu.VMEM((rows, functions), f32),
            pltpu.VMEM((2, rows, functions), bf16),
            pltpu.VMEM((2, rows, functions), bf16),
            pltpu.VMEM((4, rows, columns), bf16),
            pltpu.VMEM((4, rows, columns), bf16),
            pltpu.VMEM((3, rows, columns), bf16),
            pltpu.VMEM((3, rows, columns), bf16),
        ]
        + [pltpu.SemaphoreType.DMA((size,)) for size in (7, 3, 3, 2, 2, 4, 4, 3, 3)],
        compiler_params=pltpu.CompilerParams(
            collective_id=0, has_side_effects=True, vmem_limit_bytes=64 * 1024 * 1024
        ),
    )(
        block_home, density, points, weights.reshape(1, count), centers,
        exponents.reshape(1, functions), coefficients.reshape(1, functions),
    )


def every_block_listed(mesh, density, block_home, significant):
    shape = dict(mesh.shape)
    return (
        significant.shape[1] == block_home.shape[0] // shape["groups"]
        and (shape["blk"], shape["sub"], shape["batch"]) == (2, 2, 4)
    )


def solution(mesh):
    def whole(density, block_home, significant, *others):
        dense = every_block_listed(mesh, density, block_home, significant)
        return jax.shard_map(
            dense_body if dense else body,
            mesh=mesh,
            in_specs=(
                P(("groups", "blk", "sub"), None),
                P("groups"),
                P(("groups", "batch", "blk", "sub"), None),
                P(None, ("groups", "batch", "blk", "sub")),
                P(("groups", "batch", "blk", "sub")),
                P(None, "groups"),
                P("groups"),
                P("groups"),
            ),
            out_specs=P(("groups", "blk", "sub"), "batch"),
            check_vma=False,
        )(density, block_home, significant, *others)

    return whole
```

```python
import jax
import jax.numpy as jnp
from jax import lax
from jax.experimental import pallas as pl
from jax.experimental.pallas import tpu as pltpu
from jax.sharding import PartitionSpec as P

BATCHES = 2


SLATER = 0.7386
KAPPA = 0.804
MU_PBE = 0.2195


def energy(charge, squares):
    scaled = jnp.sqrt(charge * charge + 1.0)
    gradient_ratio = squares / scaled ** (8.0 / 3.0)
    enhance = 1.0 + KAPPA - KAPPA / (1.0 + MU_PBE * gradient_ratio / KAPPA)
    return -SLATER * scaled ** (4.0 / 3.0) * enhance


def potentials(charge, squares):
    return jax.grad(
        lambda first_arg, second_arg: jnp.sum(energy(first_arg, second_arg)), argnums=(0, 1)
    )(charge, squares)


def batch_moment(batch_points, batch_weights, center, exponent, coefficient, local_density):
    offsets = [batch_points[comp][:, None] - center[comp][None, :] for comp in range(3)]
    distance = offsets[0] * offsets[0] + offsets[1] * offsets[1] + offsets[2] * offsets[2]
    value = coefficient[None, :] * jnp.exp(-exponent[None, :] * distance)
    basis = value.astype(jnp.bfloat16)
    slopes = [
        (-2.0 * exponent[None, :] * offsets[comp] * value).astype(jnp.bfloat16) for comp in range(3)
    ]
    mixed = jnp.dot(basis, local_density, preferred_element_type=jnp.float32)
    density_value = jnp.sum(basis.astype(jnp.float32) * mixed, axis=1)
    grads = [2.0 * jnp.sum(slopes[comp].astype(jnp.float32) * mixed, axis=1) for comp in range(3)]
    gradient_sq = grads[0] * grads[0] + grads[1] * grads[1] + grads[2] * grads[2]
    pot_density, pot_gradient = potentials(density_value, gradient_sq)
    along = grads[0][:, None] * slopes[0].astype(jnp.float32)
    along = along + grads[1][:, None] * slopes[1].astype(jnp.float32)
    along = along + grads[2][:, None] * slopes[2].astype(jnp.float32)
    zeta = (
        batch_weights[:, None]
        * (
            0.5 * pot_density[:, None] * basis.astype(jnp.float32)
            + 2.0 * pot_gradient[:, None] * along
        )
    ).astype(jnp.bfloat16)
    return lax.dot_general(
        basis, zeta, (((0,), (0,)), ((), ())), preferred_element_type=jnp.float32
    )


def body(density, block_home, significant, points, weights, centers, exponents, coefficients):
    owners = lax.axis_size(("blk", "sub"))
    blocks = block_home.shape[0]
    block_width = density.shape[1] // blocks
    held = density.shape[0] // block_width
    listed = significant.shape[1]
    capacity = min(held, max(2, 2 * listed // owners))
    chosen = significant[0]
    position = block_home[chosen]
    owner_of = position // held
    local_of = position % held
    ordinal = jnp.arange(listed)
    earlier = ordinal[None, :] < ordinal[:, None]
    rank_of = jnp.sum((owner_of[None, :] == owner_of[:, None]) & earlier, axis=1)
    slot_of = owner_of * capacity + rank_of
    slot_hit = slot_of[None, :] == jnp.arange(owners * capacity)[:, None]
    asked = jnp.sum(jnp.where(slot_hit, local_of[None, :] + 1, 0), axis=1) - 1
    message = jnp.concatenate(
        [asked.reshape(owners, capacity), jnp.broadcast_to(chosen[None, :], (owners, listed))],
        axis=1,
    )
    received = lax.all_to_all(message, ("blk", "sub"), split_axis=0, concat_axis=0, tiled=True)
    wanted = received[:, :capacity]
    their_lists = received[:, capacity:]
    density_tiles = density.reshape(held, block_width, blocks, block_width)

    def pick(columns, rows_wanted):
        column_cut = jnp.take(density_tiles, columns, axis=2)
        taken = jnp.take(column_cut, jnp.maximum(rows_wanted, 0), axis=0)
        taken = jnp.where((rows_wanted >= 0)[:, None, None, None], taken, jnp.zeros_like(taken))
        return taken.reshape(capacity, block_width, listed * block_width)

    reply = jax.vmap(pick)(their_lists, wanted)
    fetched = lax.all_to_all(reply, ("blk", "sub"), split_axis=0, concat_axis=0, tiled=True)
    slots_flat = fetched.reshape(owners * capacity, block_width, listed * block_width)
    local_density = jnp.take(slots_flat, slot_of, axis=0).reshape(
        listed * block_width, listed * block_width
    )
    center = centers.reshape(3, blocks, block_width)[:, chosen, :].reshape(3, listed * block_width)
    exponent = exponents.reshape(blocks, block_width)[chosen].reshape(listed * block_width)
    coefficient = coefficients.reshape(blocks, block_width)[chosen].reshape(listed * block_width)
    batch_points = points.shape[1] // BATCHES
    moment = jnp.zeros((listed * block_width, listed * block_width), jnp.float32)
    for batch_index in range(BATCHES):
        first_point = batch_index * batch_points
        moment = moment + batch_moment(
            points[:, first_point : first_point + batch_points],
            weights[first_point : first_point + batch_points],
            center,
            exponent,
            coefficient,
            local_density,
        )
    partial_rows = (
        (moment + moment.T).astype(jnp.bfloat16).reshape(listed, block_width, listed * block_width)
    )
    entry_of = jnp.sum(jnp.where(slot_hit, ordinal[None, :] + 1, 0), axis=1) - 1
    outgoing = jnp.take(partial_rows, jnp.maximum(entry_of, 0), axis=0)
    outgoing = jnp.where((entry_of >= 0)[:, None, None], outgoing, jnp.zeros_like(outgoing))
    outgoing = outgoing.reshape(owners, capacity, block_width, listed * block_width)
    returned = lax.all_to_all(outgoing, ("blk", "sub"), split_axis=0, concat_axis=0, tiled=True)
    row_hot = (wanted[:, :, None] == jnp.arange(held)[None, None, :]).astype(jnp.bfloat16)
    grouped = jnp.einsum(
        "scl,scikj->slikj",
        row_hot,
        returned.reshape(owners, capacity, block_width, listed, block_width),
        preferred_element_type=jnp.float32,
    ).astype(jnp.bfloat16)
    column_hot = (their_lists[:, :, None] == jnp.arange(blocks)[None, None, :]).astype(jnp.bfloat16)
    summed = jnp.einsum("skn,slikj->linj", column_hot, grouped, preferred_element_type=jnp.float32)
    return lax.psum_scatter(
        summed.reshape(held * block_width, blocks * block_width),
        "batch",
        scatter_dimension=1,
        tiled=True,
    )


LOG2E = 1.4426950408889634
PAIRS = ((0, 0), (0, 1), (1, 0), (0, 2), (1, 1), (2, 0))
SINGLES = (0, 2, 5)
TERMS = 5


def three_parts(value):
    first = value.astype(jnp.bfloat16).astype(jnp.float32)
    rest = value - first
    second = rest.astype(jnp.bfloat16).astype(jnp.float32)
    third = (rest - second).astype(jnp.bfloat16).astype(jnp.float32)
    return first, second, third


def fill_rows(ref, base, rows, side):
    for term, row in enumerate(rows):
        parts = three_parts(row)
        for place, pair in enumerate(PAIRS):
            index = base + term * len(PAIRS) + place
            ref[index : index + 1, :] = parts[pair[side]]
    last = base + TERMS * len(PAIRS)
    ref[last : base + 32, :] = jnp.zeros((base + 32 - last, ref.shape[1]), jnp.float32)


def nt_dot(left, right):
    return lax.dot_general(
        left, right, (((1,), (1,)), ((), ())), preferred_element_type=jnp.float32
    )


def dense_kernel(
    home_in, density_in, points_in, weights_in, centers_in, exponents_in, coefficients_in,
    out_ref,
    home_ref, density_ref, points_ref, weights_ref, centers_ref, exponents_ref, coefficients_ref,
    place_hot, param_rows, point_rows, arg_cols, pot_cols, pot_rows,
    own_density, gathered, basis, zeta, sums, near, give_core, take_core, give_chip, take_chip,
    give_batch, take_batch,
    load_done,
    gather_send, gather_recv, core_send, core_recv, chip_send, chip_recv, batch_send, batch_recv,
):
    blk, sub, batch = lax.axis_index("blk"), lax.axis_index("sub"), lax.axis_index("batch")
    rows, functions = density_ref.shape
    blocks = home_ref.shape[0]
    width = functions // blocks
    count = points_ref.shape[1]
    columns = out_ref.shape[1]
    core_peer = {"sub": 1 - sub}
    chip_peer = {"blk": 1 - blk}
    chunk_of = [3 - batch, (batch + 2) % 4, batch + 1 - 2 * (batch % 2), batch]
    batch_peers = [{"batch": chunk_of[k]} for k in range(3)]

    barrier = pltpu.get_barrier_semaphore()
    for peer in [core_peer, chip_peer] + batch_peers:
        pl.semaphore_signal(barrier, inc=1, device_id=peer, device_id_type=pl.DeviceIdType.MESH)

    loads = []
    for source, target in (
        (home_in, home_ref), (density_in, density_ref), (centers_in, centers_ref),
        (exponents_in, exponents_ref), (coefficients_in, coefficients_ref),
        (points_in, points_ref), (weights_in, weights_ref),
    ):
        copy = pltpu.make_async_copy(source, target, load_done.at[len(loads)])
        copy.start()
        loads.append(copy)

    gap = lax.broadcasted_iota(jnp.int32, (width, functions), 1) - lax.broadcasted_iota(
        jnp.int32, (width, functions), 0
    )
    loads[0].wait()
    for index in range(blocks):
        place_hot[index * width : (index + 1) * width, :] = jnp.where(
            gap == home_ref[index] * width, 1.0, 0.0
        ).astype(jnp.bfloat16)
    loads[1].wait()
    own_density[...] = jnp.dot(
        density_ref[...], place_hot[...], preferred_element_type=jnp.float32
    ).astype(jnp.bfloat16)

    pl.semaphore_wait(barrier, 5)

    def remote(source, target, send, recv, peer):
        return pltpu.make_async_remote_copy(
            src_ref=source, dst_ref=target, send_sem=send, recv_sem=recv,
            device_id=peer, device_id_type=pl.DeviceIdType.MESH,
        )

    to_chip = remote(own_density, gathered.at[1], gather_send.at[1], gather_recv.at[1], chip_peer)
    to_core = remote(own_density, gathered.at[0], gather_send.at[0], gather_recv.at[0], core_peer)
    forward = remote(gathered.at[1], gathered.at[2], gather_send.at[2], gather_recv.at[2], core_peer)
    to_chip.start()
    to_core.start()

    for copy in loads[2:]:
        copy.wait()
    exponent = exponents_ref[...]
    center = [centers_ref[comp : comp + 1, :] for comp in range(3)]
    point = [points_ref[comp : comp + 1, :] for comp in range(3)]
    scaled = exponent * LOG2E
    norm = center[0] * center[0] + center[1] * center[1] + center[2] * center[2]
    constant = jnp.log(coefficients_ref[...]) * LOG2E - scaled * norm
    fill_rows(
        param_rows, 0, [constant] + [2.0 * scaled * center[comp] for comp in range(3)] + [-scaled], 0
    )
    fill_rows(
        param_rows, 32,
        [jnp.ones_like(exponent), exponent] + [exponent * center[comp] for comp in range(3)], 0,
    )
    radius = point[0] * point[0] + point[1] * point[1] + point[2] * point[2]
    fill_rows(point_rows, 0, [jnp.ones_like(radius)] + point + [radius], 1)
    placed = jnp.dot(
        param_rows[...].astype(jnp.bfloat16), place_hot[...], preferred_element_type=jnp.float32
    )
    arg_cols[...] = jnp.transpose(placed[0:32, :]).astype(jnp.bfloat16)
    pot_cols[...] = jnp.transpose(placed[32:64, :]).astype(jnp.bfloat16)
    pot_rows[...] = placed[32:64, :].astype(jnp.bfloat16)

    piece = 512
    point_parts = point_rows[...].astype(jnp.bfloat16)
    for row in range(0, functions, rows):
        for column in range(0, count, piece):
            argument = jnp.dot(
                arg_cols[row : row + rows, :], point_parts[:, column : column + piece],
                preferred_element_type=jnp.float32,
            )
            basis[row : row + rows, column : column + piece] = jnp.exp2(argument).astype(
                jnp.bfloat16
            )

    def owner_rows(owner):
        return pl.ds(pl.multiple_of(owner * rows, rows), rows)

    def both(ref, owners, lanes):
        return jnp.concatenate([ref[owner_rows(owner), lanes] for owner in owners], axis=0)

    def accumulate(stage, first_rows, second_rows, owners):
        held_rows = jnp.concatenate([first_rows, second_rows], axis=0)
        own = jnp.concatenate([pot_rows[:, owner_rows(owner)] for owner in owners], axis=1)
        for column in range(0, count, piece):
            lanes = slice(column, column + piece)
            mixed = jnp.dot(held_rows, basis[:, lanes], preferred_element_type=jnp.float32)
            value = both(basis, owners, lanes).astype(jnp.float32)
            total = jnp.dot(
                own, (mixed * value).astype(jnp.bfloat16), preferred_element_type=jnp.float32
            )
            if stage > 0:
                total = total + sums[:, lanes]
            sums[:, lanes] = total

    to_core.wait_recv()
    accumulate(0, own_density[...], gathered[0], (blk * 2 + sub, blk * 2 + 1 - sub))
    to_chip.wait_recv()
    forward.start()
    forward.wait_recv()
    accumulate(1, gathered[1], gathered[2], ((1 - blk) * 2 + sub, (1 - blk) * 2 + 1 - sub))

    moments = []
    for term in range(TERMS):
        base = term * len(PAIRS)
        moment = sums[base : base + 1, :]
        for place in SINGLES[1:]:
            moment = moment + sums[base + place : base + place + 1, :]
        moments.append(moment)
    charge = moments[0]
    grads = [-4.0 * (point[comp] * moments[1] - moments[2 + comp]) for comp in range(3)]
    squares = grads[0] * grads[0] + grads[1] * grads[1] + grads[2] * grads[2]
    shrink = jnp.exp(jnp.log(charge * charge + 1.0) * (-1.0 / 3.0))
    shrink_sq = shrink * shrink
    ratio = squares * shrink_sq * shrink_sq
    inner = 1.0 / (1.0 + (MU_PBE / KAPPA) * ratio)
    enhance = 1.0 + KAPPA - KAPPA * inner
    slope = MU_PBE * ratio * inner * inner
    pot_density = -SLATER * charge * shrink * ((4.0 / 3.0) * enhance - (8.0 / 3.0) * slope)
    pot_gradient = -SLATER * MU_PBE * shrink_sq * inner * inner
    weight = weights_ref[...]
    lean = [4.0 * weight * pot_gradient * grads[comp] for comp in range(3)]
    along = -(lean[0] * point[0] + lean[1] * point[1] + lean[2] * point[2])
    fill_rows(point_rows, 0, [0.5 * weight * pot_density, along] + lean, 1)
    pot_parts = point_rows[...].astype(jnp.bfloat16)
    for row in range(0, functions, rows):
        for column in range(0, count, piece):
            factor = jnp.dot(
                pot_cols[row : row + rows, :], pot_parts[:, column : column + piece],
                preferred_element_type=jnp.float32,
            )
            value = basis[row : row + rows, column : column + piece].astype(jnp.float32)
            zeta[row : row + rows, column : column + piece] = (value * factor).astype(jnp.bfloat16)

    every = slice(0, count)

    def partial_rows(owners):
        product = nt_dot(both(basis, owners, every), zeta[...]) + nt_dot(
            both(zeta, owners, every), basis[...]
        )
        return nt_dot(product.astype(jnp.bfloat16), place_hot[...])

    core_copies, chip_copies, batch_copies = [], [], []
    sent = partial_rows(((1 - blk) * 2 + 1 - sub, blk * 2 + 1 - sub)).astype(jnp.bfloat16)
    for turn in range(2):
        give_core[turn] = sent[turn * rows : (turn + 1) * rows]
        copy = remote(
            give_core.at[turn], take_core.at[turn], core_send.at[turn], core_recv.at[turn], core_peer
        )
        copy.start()
        core_copies.append(copy)
    near[...] = partial_rows(((1 - blk) * 2 + sub, blk * 2 + sub))
    core_copies[0].wait_recv()
    for chunk in range(4):
        lanes = pl.ds(pl.multiple_of(chunk_of[chunk] * columns, columns), columns)
        give_chip[chunk] = (near[:rows, lanes] + take_core[0, :, lanes].astype(jnp.float32)).astype(
            jnp.bfloat16
        )
        copy = remote(
            give_chip.at[chunk], take_chip.at[chunk], chip_send.at[chunk], chip_recv.at[chunk],
            chip_peer,
        )
        copy.start()
        chip_copies.append(copy)
    core_copies[1].wait_recv()
    for chunk in range(4):
        lanes = pl.ds(pl.multiple_of(chunk_of[chunk] * columns, columns), columns)
        total = near[rows:, lanes] + take_core[1, :, lanes].astype(jnp.float32)
        chip_copies[chunk].wait_recv()
        total = total + take_chip[chunk].astype(jnp.float32)
        if chunk < 3:
            give_batch[chunk] = total.astype(jnp.bfloat16)
            copy = remote(
                give_batch.at[chunk], take_batch.at[chunk], batch_send.at[chunk],
                batch_recv.at[chunk], batch_peers[chunk],
            )
            copy.start()
            batch_copies.append(copy)
    for chunk in (2, 1, 0):
        batch_copies[chunk].wait_recv()
        total = total + take_batch[chunk].astype(jnp.float32)
    out_ref[...] = total
    for copy in [to_chip, to_core, forward] + core_copies + chip_copies + batch_copies:
        copy.wait_send()


def dense_body(density, block_home, significant, points, weights, centers, exponents, coefficients):
    rows, functions = density.shape
    count = points.shape[1]
    columns = functions // 4
    f32, bf16 = jnp.float32, jnp.bfloat16
    vmem = pl.BlockSpec(memory_space=pltpu.VMEM)
    return pl.pallas_call(
        dense_kernel,
        out_shape=jax.ShapeDtypeStruct((rows, columns), f32),
        in_specs=[pl.BlockSpec(memory_space=pltpu.HBM)] * 7,
        out_specs=vmem,
        scratch_shapes=[
            pltpu.SMEM(block_home.shape, jnp.int32),
            pltpu.VMEM((rows, functions), bf16),
            pltpu.VMEM((3, count), f32),
            pltpu.VMEM((1, count), f32),
            pltpu.VMEM((3, functions), f32),
            pltpu.VMEM((1, functions), f32),
            pltpu.VMEM((1, functions), f32),
            pltpu.VMEM((functions, functions), bf16),
            pltpu.VMEM((64, functions), f32),
            pltpu.VMEM((32, count), f32),
            pltpu.VMEM((functions, 32), bf16),
            pltpu.VMEM((functions, 32), bf16),
            pltpu.VMEM((32, functions), bf16),
            pltpu.VMEM((rows, functions), bf16),
            pltpu.VMEM((3, rows, functions), bf16),
            pltpu.VMEM((functions, count), bf16),
            pltpu.VMEM((functions, count), bf16),
            pltpu.VMEM((32, count), f32),
            pltpu.VMEM((2 * rows, functions), f32),
            pltpu.VMEM((2, rows, functions), bf16),
            pltpu.VMEM((2, rows, functions), bf16),
            pltpu.VMEM((4, rows, columns), bf16),
            pltpu.VMEM((4, rows, columns), bf16),
            pltpu.VMEM((3, rows, columns), bf16),
            pltpu.VMEM((3, rows, columns), bf16),
        ]
        + [pltpu.SemaphoreType.DMA((size,)) for size in (7, 3, 3, 2, 2, 4, 4, 3, 3)],
        compiler_params=pltpu.CompilerParams(
            collective_id=0, has_side_effects=True, vmem_limit_bytes=64 * 1024 * 1024
        ),
    )(
        block_home, density, points, weights.reshape(1, count), centers,
        exponents.reshape(1, functions), coefficients.reshape(1, functions),
    )


def every_block_listed(mesh, density, block_home, significant):
    shape = dict(mesh.shape)
    return (
        significant.shape[1] == block_home.shape[0] // shape["groups"]
        and (shape["blk"], shape["sub"], shape["batch"]) == (2, 2, 4)
    )


def solution(mesh):
    def whole(density, block_home, significant, *others):
        dense = every_block_listed(mesh, density, block_home, significant)
        return jax.shard_map(
            dense_body if dense else body,
            mesh=mesh,
            in_specs=(
                P(("groups", "blk", "sub"), None),
                P("groups"),
                P(("groups", "batch", "blk", "sub"), None),
                P(None, ("groups", "batch", "blk", "sub")),
                P(("groups", "batch", "blk", "sub")),
                P(None, "groups"),
                P("groups"),
                P("groups"),
            ),
            out_specs=P(("groups", "blk", "sub"), "batch"),
            check_vma=False,
        )(density, block_home, significant, *others)

    return whole
```

```python
import jax
import jax.numpy as jnp
from jax import lax
from jax.experimental import pallas as pl
from jax.experimental.pallas import tpu as pltpu
from jax.sharding import PartitionSpec as P

BATCHES = 2


SLATER = 0.7386
KAPPA = 0.804
MU_PBE = 0.2195


def energy(charge, squares):
    scaled = jnp.sqrt(charge * charge + 1.0)
    gradient_ratio = squares / scaled ** (8.0 / 3.0)
    enhance = 1.0 + KAPPA - KAPPA / (1.0 + MU_PBE * gradient_ratio / KAPPA)
    return -SLATER * scaled ** (4.0 / 3.0) * enhance


def potentials(charge, squares):
    return jax.grad(
        lambda first_arg, second_arg: jnp.sum(energy(first_arg, second_arg)), argnums=(0, 1)
    )(charge, squares)


def batch_moment(batch_points, batch_weights, center, exponent, coefficient, local_density):
    offsets = [batch_points[comp][:, None] - center[comp][None, :] for comp in range(3)]
    distance = offsets[0] * offsets[0] + offsets[1] * offsets[1] + offsets[2] * offsets[2]
    value = coefficient[None, :] * jnp.exp(-exponent[None, :] * distance)
    basis = value.astype(jnp.bfloat16)
    slopes = [
        (-2.0 * exponent[None, :] * offsets[comp] * value).astype(jnp.bfloat16) for comp in range(3)
    ]
    mixed = jnp.dot(basis, local_density, preferred_element_type=jnp.float32)
    density_value = jnp.sum(basis.astype(jnp.float32) * mixed, axis=1)
    grads = [2.0 * jnp.sum(slopes[comp].astype(jnp.float32) * mixed, axis=1) for comp in range(3)]
    gradient_sq = grads[0] * grads[0] + grads[1] * grads[1] + grads[2] * grads[2]
    pot_density, pot_gradient = potentials(density_value, gradient_sq)
    along = grads[0][:, None] * slopes[0].astype(jnp.float32)
    along = along + grads[1][:, None] * slopes[1].astype(jnp.float32)
    along = along + grads[2][:, None] * slopes[2].astype(jnp.float32)
    zeta = (
        batch_weights[:, None]
        * (
            0.5 * pot_density[:, None] * basis.astype(jnp.float32)
            + 2.0 * pot_gradient[:, None] * along
        )
    ).astype(jnp.bfloat16)
    return lax.dot_general(
        basis, zeta, (((0,), (0,)), ((), ())), preferred_element_type=jnp.float32
    )


def body(density, block_home, significant, points, weights, centers, exponents, coefficients):
    owners = lax.axis_size(("blk", "sub"))
    blocks = block_home.shape[0]
    block_width = density.shape[1] // blocks
    held = density.shape[0] // block_width
    listed = significant.shape[1]
    capacity = min(held, max(2, 2 * listed // owners))
    chosen = significant[0]
    position = block_home[chosen]
    owner_of = position // held
    local_of = position % held
    ordinal = jnp.arange(listed)
    earlier = ordinal[None, :] < ordinal[:, None]
    rank_of = jnp.sum((owner_of[None, :] == owner_of[:, None]) & earlier, axis=1)
    slot_of = owner_of * capacity + rank_of
    slot_hit = slot_of[None, :] == jnp.arange(owners * capacity)[:, None]
    asked = jnp.sum(jnp.where(slot_hit, local_of[None, :] + 1, 0), axis=1) - 1
    message = jnp.concatenate(
        [asked.reshape(owners, capacity), jnp.broadcast_to(chosen[None, :], (owners, listed))],
        axis=1,
    )
    received = lax.all_to_all(message, ("blk", "sub"), split_axis=0, concat_axis=0, tiled=True)
    wanted = received[:, :capacity]
    their_lists = received[:, capacity:]
    density_tiles = density.reshape(held, block_width, blocks, block_width)

    def pick(columns, rows_wanted):
        column_cut = jnp.take(density_tiles, columns, axis=2)
        taken = jnp.take(column_cut, jnp.maximum(rows_wanted, 0), axis=0)
        taken = jnp.where((rows_wanted >= 0)[:, None, None, None], taken, jnp.zeros_like(taken))
        return taken.reshape(capacity, block_width, listed * block_width)

    reply = jax.vmap(pick)(their_lists, wanted)
    fetched = lax.all_to_all(reply, ("blk", "sub"), split_axis=0, concat_axis=0, tiled=True)
    slots_flat = fetched.reshape(owners * capacity, block_width, listed * block_width)
    local_density = jnp.take(slots_flat, slot_of, axis=0).reshape(
        listed * block_width, listed * block_width
    )
    center = centers.reshape(3, blocks, block_width)[:, chosen, :].reshape(3, listed * block_width)
    exponent = exponents.reshape(blocks, block_width)[chosen].reshape(listed * block_width)
    coefficient = coefficients.reshape(blocks, block_width)[chosen].reshape(listed * block_width)
    batch_points = points.shape[1] // BATCHES
    moment = jnp.zeros((listed * block_width, listed * block_width), jnp.float32)
    for batch_index in range(BATCHES):
        first_point = batch_index * batch_points
        moment = moment + batch_moment(
            points[:, first_point : first_point + batch_points],
            weights[first_point : first_point + batch_points],
            center,
            exponent,
            coefficient,
            local_density,
        )
    partial_rows = (
        (moment + moment.T).astype(jnp.bfloat16).reshape(listed, block_width, listed * block_width)
    )
    entry_of = jnp.sum(jnp.where(slot_hit, ordinal[None, :] + 1, 0), axis=1) - 1
    outgoing = jnp.take(partial_rows, jnp.maximum(entry_of, 0), axis=0)
    outgoing = jnp.where((entry_of >= 0)[:, None, None], outgoing, jnp.zeros_like(outgoing))
    outgoing = outgoing.reshape(owners, capacity, block_width, listed * block_width)
    returned = lax.all_to_all(outgoing, ("blk", "sub"), split_axis=0, concat_axis=0, tiled=True)
    row_hot = (wanted[:, :, None] == jnp.arange(held)[None, None, :]).astype(jnp.bfloat16)
    grouped = jnp.einsum(
        "scl,scikj->slikj",
        row_hot,
        returned.reshape(owners, capacity, block_width, listed, block_width),
        preferred_element_type=jnp.float32,
    ).astype(jnp.bfloat16)
    column_hot = (their_lists[:, :, None] == jnp.arange(blocks)[None, None, :]).astype(jnp.bfloat16)
    summed = jnp.einsum("skn,slikj->linj", column_hot, grouped, preferred_element_type=jnp.float32)
    return lax.psum_scatter(
        summed.reshape(held * block_width, blocks * block_width),
        "batch",
        scatter_dimension=1,
        tiled=True,
    )


LOG2E = 1.4426950408889634
PAIRS = ((0, 0), (0, 1), (1, 0), (0, 2), (1, 1), (2, 0))
SINGLES = (0, 2, 5)
TERMS = 5


def three_parts(value):
    first = value.astype(jnp.bfloat16).astype(jnp.float32)
    rest = value - first
    second = rest.astype(jnp.bfloat16).astype(jnp.float32)
    third = (rest - second).astype(jnp.bfloat16).astype(jnp.float32)
    return first, second, third


def fill_rows(ref, base, rows, side):
    for term, row in enumerate(rows):
        parts = three_parts(row)
        for place, pair in enumerate(PAIRS):
            index = base + term * len(PAIRS) + place
            ref[index : index + 1, :] = parts[pair[side]]
    last = base + TERMS * len(PAIRS)
    ref[last : base + 32, :] = jnp.zeros((base + 32 - last, ref.shape[1]), jnp.float32)


def nt_dot(left, right):
    return lax.dot_general(
        left, right, (((1,), (1,)), ((), ())), preferred_element_type=jnp.float32
    )


def dense_kernel(
    home_in, density_in, points_in, weights_in, centers_in, exponents_in, coefficients_in,
    out_ref,
    home_ref, density_ref, points_ref, weights_ref, centers_ref, exponents_ref, coefficients_ref,
    place_hot, param_rows, point_rows, arg_cols, pot_cols, pot_rows,
    own_density, gathered, basis, zeta, sums, whole, near, give_core, take_core, give_chip, take_chip,
    give_batch, take_batch,
    load_done,
    gather_send, gather_recv, core_send, core_recv, chip_send, chip_recv, batch_send, batch_recv,
):
    blk, sub, batch = lax.axis_index("blk"), lax.axis_index("sub"), lax.axis_index("batch")
    rows, functions = density_ref.shape
    blocks = home_ref.shape[0]
    width = functions // blocks
    count = points_ref.shape[1]
    columns = out_ref.shape[1]
    core_peer = {"sub": 1 - sub}
    chip_peer = {"blk": 1 - blk}
    chunk_of = [3 - batch, (batch + 2) % 4, batch + 1 - 2 * (batch % 2), batch]
    batch_peers = [{"batch": chunk_of[k]} for k in range(3)]

    barrier = pltpu.get_barrier_semaphore()
    for peer in [core_peer, chip_peer] + batch_peers:
        pl.semaphore_signal(barrier, inc=1, device_id=peer, device_id_type=pl.DeviceIdType.MESH)

    loads = []
    for source, target in (
        (home_in, home_ref), (density_in, density_ref), (centers_in, centers_ref),
        (exponents_in, exponents_ref), (coefficients_in, coefficients_ref),
        (points_in, points_ref), (weights_in, weights_ref),
    ):
        copy = pltpu.make_async_copy(source, target, load_done.at[len(loads)])
        copy.start()
        loads.append(copy)

    gap = lax.broadcasted_iota(jnp.int32, (width, functions), 1) - lax.broadcasted_iota(
        jnp.int32, (width, functions), 0
    )
    loads[0].wait()
    for index in range(blocks):
        place_hot[index * width : (index + 1) * width, :] = jnp.where(
            gap == home_ref[index] * width, 1.0, 0.0
        ).astype(jnp.bfloat16)
    loads[1].wait()
    own_density[...] = jnp.dot(
        density_ref[...], place_hot[...], preferred_element_type=jnp.float32
    ).astype(jnp.bfloat16)

    pl.semaphore_wait(barrier, 5)

    def remote(source, target, send, recv, peer):
        return pltpu.make_async_remote_copy(
            src_ref=source, dst_ref=target, send_sem=send, recv_sem=recv,
            device_id=peer, device_id_type=pl.DeviceIdType.MESH,
        )

    to_chip = remote(own_density, gathered.at[1], gather_send.at[1], gather_recv.at[1], chip_peer)
    to_core = remote(own_density, gathered.at[0], gather_send.at[0], gather_recv.at[0], core_peer)
    forward = remote(gathered.at[1], gathered.at[2], gather_send.at[2], gather_recv.at[2], core_peer)
    to_chip.start()
    to_core.start()

    for copy in loads[2:]:
        copy.wait()
    exponent = exponents_ref[...]
    center = [centers_ref[comp : comp + 1, :] for comp in range(3)]
    point = [points_ref[comp : comp + 1, :] for comp in range(3)]
    scaled = exponent * LOG2E
    norm = center[0] * center[0] + center[1] * center[1] + center[2] * center[2]
    constant = jnp.log(coefficients_ref[...]) * LOG2E - scaled * norm
    fill_rows(
        param_rows, 0, [constant] + [2.0 * scaled * center[comp] for comp in range(3)] + [-scaled], 0
    )
    fill_rows(
        param_rows, 32,
        [jnp.ones_like(exponent), exponent] + [exponent * center[comp] for comp in range(3)], 0,
    )
    radius = point[0] * point[0] + point[1] * point[1] + point[2] * point[2]
    fill_rows(point_rows, 0, [jnp.ones_like(radius)] + point + [radius], 1)
    placed = jnp.dot(
        param_rows[...].astype(jnp.bfloat16), place_hot[...], preferred_element_type=jnp.float32
    )
    arg_cols[...] = jnp.transpose(placed[0:32, :]).astype(jnp.bfloat16)
    pot_cols[...] = jnp.transpose(placed[32:64, :]).astype(jnp.bfloat16)
    pot_rows[...] = placed[32:64, :].astype(jnp.bfloat16)

    piece = 512
    point_parts = point_rows[...].astype(jnp.bfloat16)
    for row in range(0, functions, rows):
        for column in range(0, count, piece):
            argument = jnp.dot(
                arg_cols[row : row + rows, :], point_parts[:, column : column + piece],
                preferred_element_type=jnp.float32,
            )
            basis[row : row + rows, column : column + piece] = jnp.exp2(argument).astype(
                jnp.bfloat16
            )

    def owner_rows(owner):
        return pl.ds(pl.multiple_of(owner * rows, rows), rows)

    def both(ref, owners, lanes):
        return jnp.concatenate([ref[owner_rows(owner), lanes] for owner in owners], axis=0)

    def accumulate(stage, first_rows, second_rows, owners):
        held_rows = jnp.concatenate([first_rows, second_rows], axis=0)
        own = jnp.concatenate([pot_rows[:, owner_rows(owner)] for owner in owners], axis=1)
        for column in range(0, count, piece):
            lanes = slice(column, column + piece)
            mixed = jnp.dot(held_rows, basis[:, lanes], preferred_element_type=jnp.float32)
            value = both(basis, owners, lanes).astype(jnp.float32)
            total = jnp.dot(
                own, (mixed * value).astype(jnp.bfloat16), preferred_element_type=jnp.float32
            )
            if stage > 0:
                total = total + sums[:, lanes]
            sums[:, lanes] = total

    to_core.wait_recv()
    accumulate(0, own_density[...], gathered[0], (blk * 2 + sub, blk * 2 + 1 - sub))
    to_chip.wait_recv()
    forward.start()
    forward.wait_recv()
    accumulate(1, gathered[1], gathered[2], ((1 - blk) * 2 + sub, (1 - blk) * 2 + 1 - sub))

    moments = []
    for term in range(TERMS):
        base = term * len(PAIRS)
        moment = sums[base : base + 1, :]
        for place in SINGLES[1:]:
            moment = moment + sums[base + place : base + place + 1, :]
        moments.append(moment)
    charge = moments[0]
    grads = [-4.0 * (point[comp] * moments[1] - moments[2 + comp]) for comp in range(3)]
    squares = grads[0] * grads[0] + grads[1] * grads[1] + grads[2] * grads[2]
    shrink = jnp.exp(jnp.log(charge * charge + 1.0) * (-1.0 / 3.0))
    shrink_sq = shrink * shrink
    ratio = squares * shrink_sq * shrink_sq
    inner = 1.0 / (1.0 + (MU_PBE / KAPPA) * ratio)
    enhance = 1.0 + KAPPA - KAPPA * inner
    slope = MU_PBE * ratio * inner * inner
    pot_density = -SLATER * charge * shrink * ((4.0 / 3.0) * enhance - (8.0 / 3.0) * slope)
    pot_gradient = -SLATER * MU_PBE * shrink_sq * inner * inner
    weight = weights_ref[...]
    lean = [4.0 * weight * pot_gradient * grads[comp] for comp in range(3)]
    along = -(lean[0] * point[0] + lean[1] * point[1] + lean[2] * point[2])
    fill_rows(point_rows, 0, [0.5 * weight * pot_density, along] + lean, 1)
    pot_parts = point_rows[...].astype(jnp.bfloat16)
    for row in range(0, functions, rows):
        for column in range(0, count, piece):
            factor = jnp.dot(
                pot_cols[row : row + rows, :], pot_parts[:, column : column + piece],
                preferred_element_type=jnp.float32,
            )
            value = basis[row : row + rows, column : column + piece].astype(jnp.float32)
            zeta[row : row + rows, column : column + piece] = (value * factor).astype(jnp.bfloat16)

    moment = nt_dot(basis[...], zeta[...])
    whole[...] = (moment + jnp.transpose(moment)).astype(jnp.bfloat16)
    every = slice(0, functions)

    def partial_rows(owners):
        return nt_dot(both(whole, owners, every), place_hot[...])

    core_copies, chip_copies, batch_copies = [], [], []
    sent = partial_rows(((1 - blk) * 2 + 1 - sub, blk * 2 + 1 - sub)).astype(jnp.bfloat16)
    for turn in range(2):
        give_core[turn] = sent[turn * rows : (turn + 1) * rows]
        copy = remote(
            give_core.at[turn], take_core.at[turn], core_send.at[turn], core_recv.at[turn], core_peer
        )
        copy.start()
        core_copies.append(copy)
    near[...] = partial_rows(((1 - blk) * 2 + sub, blk * 2 + sub))
    core_copies[0].wait_recv()
    for chunk in range(4):
        lanes = pl.ds(pl.multiple_of(chunk_of[chunk] * columns, columns), columns)
        give_chip[chunk] = (near[:rows, lanes] + take_core[0, :, lanes].astype(jnp.float32)).astype(
            jnp.bfloat16
        )
        copy = remote(
            give_chip.at[chunk], take_chip.at[chunk], chip_send.at[chunk], chip_recv.at[chunk],
            chip_peer,
        )
        copy.start()
        chip_copies.append(copy)
    core_copies[1].wait_recv()
    for chunk in range(4):
        lanes = pl.ds(pl.multiple_of(chunk_of[chunk] * columns, columns), columns)
        total = near[rows:, lanes] + take_core[1, :, lanes].astype(jnp.float32)
        chip_copies[chunk].wait_recv()
        total = total + take_chip[chunk].astype(jnp.float32)
        if chunk < 3:
            give_batch[chunk] = total.astype(jnp.bfloat16)
            copy = remote(
                give_batch.at[chunk], take_batch.at[chunk], batch_send.at[chunk],
                batch_recv.at[chunk], batch_peers[chunk],
            )
            copy.start()
            batch_copies.append(copy)
    for chunk in (2, 1, 0):
        batch_copies[chunk].wait_recv()
        total = total + take_batch[chunk].astype(jnp.float32)
    out_ref[...] = total
    for copy in [to_chip, to_core, forward] + core_copies + chip_copies + batch_copies:
        copy.wait_send()


def dense_body(density, block_home, significant, points, weights, centers, exponents, coefficients):
    rows, functions = density.shape
    count = points.shape[1]
    columns = functions // 4
    f32, bf16 = jnp.float32, jnp.bfloat16
    vmem = pl.BlockSpec(memory_space=pltpu.VMEM)
    return pl.pallas_call(
        dense_kernel,
        out_shape=jax.ShapeDtypeStruct((rows, columns), f32),
        in_specs=[pl.BlockSpec(memory_space=pltpu.HBM)] * 7,
        out_specs=vmem,
        scratch_shapes=[
            pltpu.SMEM(block_home.shape, jnp.int32),
            pltpu.VMEM((rows, functions), bf16),
            pltpu.VMEM((3, count), f32),
            pltpu.VMEM((1, count), f32),
            pltpu.VMEM((3, functions), f32),
            pltpu.VMEM((1, functions), f32),
            pltpu.VMEM((1, functions), f32),
            pltpu.VMEM((functions, functions), bf16),
            pltpu.VMEM((64, functions), f32),
            pltpu.VMEM((32, count), f32),
            pltpu.VMEM((functions, 32), bf16),
            pltpu.VMEM((functions, 32), bf16),
            pltpu.VMEM((32, functions), bf16),
            pltpu.VMEM((rows, functions), bf16),
            pltpu.VMEM((3, rows, functions), bf16),
            pltpu.VMEM((functions, count), bf16),
            pltpu.VMEM((functions, count), bf16),
            pltpu.VMEM((32, count), f32),
            pltpu.VMEM((functions, functions), bf16),
            pltpu.VMEM((2 * rows, functions), f32),
            pltpu.VMEM((2, rows, functions), bf16),
            pltpu.VMEM((2, rows, functions), bf16),
            pltpu.VMEM((4, rows, columns), bf16),
            pltpu.VMEM((4, rows, columns), bf16),
            pltpu.VMEM((3, rows, columns), bf16),
            pltpu.VMEM((3, rows, columns), bf16),
        ]
        + [pltpu.SemaphoreType.DMA((size,)) for size in (7, 3, 3, 2, 2, 4, 4, 3, 3)],
        compiler_params=pltpu.CompilerParams(
            collective_id=0, has_side_effects=True, vmem_limit_bytes=64 * 1024 * 1024
        ),
    )(
        block_home, density, points, weights.reshape(1, count), centers,
        exponents.reshape(1, functions), coefficients.reshape(1, functions),
    )


def every_block_listed(mesh, density, block_home, significant):
    shape = dict(mesh.shape)
    return (
        significant.shape[1] == block_home.shape[0] // shape["groups"]
        and (shape["blk"], shape["sub"], shape["batch"]) == (2, 2, 4)
    )


def solution(mesh):
    def whole(density, block_home, significant, *others):
        dense = every_block_listed(mesh, density, block_home, significant)
        return jax.shard_map(
            dense_body if dense else body,
            mesh=mesh,
            in_specs=(
                P(("groups", "blk", "sub"), None),
                P("groups"),
                P(("groups", "batch", "blk", "sub"), None),
                P(None, ("groups", "batch", "blk", "sub")),
                P(("groups", "batch", "blk", "sub")),
                P(None, "groups"),
                P("groups"),
                P("groups"),
            ),
            out_specs=P(("groups", "blk", "sub"), "batch"),
            check_vma=False,
        )(density, block_home, significant, *others)

    return whole
```
